32 devices in a mesh: group: 2 (over x), date: 16 (over z, y, core).
Axes of the slice: x: 2, y: 2, z: 4, core: 2. Of those that a mesh axis runs over, the one named last changes fastest.
Arguments:
- salvo_records: bfloat16 [32, 3, 2, 13, 1024], P(('group', 'date')), parts along dimension 0, may hold values from -6 to 6
- stencil_weights: bfloat16 [32, 3, 8], P(('group', 'date')), parts along dimension 0, may hold values from -2 to 2
- zone_drifts: int32 [32, 3], P(('group', 'date')), parts along dimension 0, may hold values from -16 to 16
- seam_sweeps: int32 [32, 2], P(('group', 'date')), parts along dimension 0, may hold values from 1 to 2
- prior_sweeps: int32 [32], P(('group', 'date')), parts along dimension 0, may hold values from 0 to 1
- viewing_frames: int32 [512, 128], P(('group', 'date')), parts along dimension 0, may hold values from 0 to 4095, as said below
Outputs:
- filtered: bfloat16 [32, 2, 32, 1024], P(('group', 'date')), parts along dimension 0
The draws below stay inside these ranges and needn't reach their ends.
There are 2 independent parts, one for each index of `group`. The reference program is written for one: setup_inputs(seed, part) draws one part's arguments, and reference() takes and returns one part's arrays. A program takes and returns all parts, laid end to end along the dimension named above; each array names one. Nothing has to cross between parts.
Inputs may be any that keep to these rules, and one draw needn't show every extreme that they name: `viewing_frames`: window w belongs to ground block g = w // 16 and names pixels line-major among 4 lines of 1024 cells: local line 0 is the line above the block, lines 1 .. 2 the block, line 3 the line below. The first block never names local line 0, the last block never names local line 3.
All inputs are finite; a program needn't handle non-finite values.
Results may differ from the reference program's by a relative error of at most 0.019.
Values may be sent and summed in bfloat16 or wider, within the bound.
A program may use at most 64 MiB of HBM per device.

```python
import math
import jax
import jax.numpy as jnp
from jax import lax

LB = 2
DISTANCE_BINS = 1024
SALVO_TALLY = 3
STENCIL_WEIGHTS = 8
BAND_DRIFT_LIMIT = 16
LOOKS = 128
ITERS = 8
PATCH = 32
CAPTURE_TALLY = 16
FLIGHT_SWEEPS = 32
JOINT_SWEEPS_TOP = 2
JOINT_SWEEPS_LOW = 1
OFF = 1
SALVO_SWEEPS = 13
WIN_DEV = 16
WINDOWS = 256
N_DATE = 16


def draw_viewing_frames(key, part):
    extent = (LB + 2) * DISTANCE_BINS
    chosen = jax.random.randint(key, (WINDOWS, LOOKS), 0, extent).astype(jnp.int32)
    block_of = (jnp.arange(WINDOWS, dtype=jnp.int32) // WIN_DEV)[:, None]
    line_of = chosen // DISTANCE_BINS
    last_block = WINDOWS // WIN_DEV - 1
    chosen = jnp.where((block_of == 0) & (line_of == 0), chosen + DISTANCE_BINS, chosen)
    chosen = jnp.where((block_of == last_block) & (line_of == LB + 1), chosen - DISTANCE_BINS, chosen)
    chosen = chosen.at[0, 0].set(extent - 1)
    chosen = chosen.at[WIN_DEV, 0].set(0)
    return chosen.astype(jnp.int32)


def touch_ends(values, rng, smallest, largest):
    shape = values.shape
    place = [jax.random.randint(jax.random.fold_in(rng, axis), (), 0, shape[axis]) for axis in range(len(shape))]
    values = values.at[tuple(place)].set(smallest)
    longest = shape.index(max(shape))
    place[longest] = (place[longest] + 1) % shape[longest]
    return values.at[tuple(place)].set(largest)


def level_of(key, dims, split, least, largest):
    level, own = 1.0, jax.random.fold_in(key, 6)
    for dim, shards_of in split:
        steps = jnp.exp(jax.random.uniform(jax.random.fold_in(own, dim), (shards_of,), jnp.float32, least / len(split), largest / len(split)))
        level = level * jnp.repeat(steps, dims[dim] // shards_of).reshape([-1 if axis == dim else 1 for axis in range(len(dims))])
    return level


def centred(own_key, shape, deviation, bound, pieces=(), kind=jnp.bfloat16):
    entries = deviation * jax.random.normal(own_key, shape, jnp.float32)
    if pieces:
        entries = entries * level_of(own_key, shape, pieces, -0.22, 0.18)
    return jnp.clip(entries, -bound, bound).astype(kind)


def setup_inputs(seed: int = 0, part: int = 0) -> dict:
    seeds = jax.random.split(jax.random.key(seed), 7)
    part_splits = jax.random.split(jax.random.fold_in(seeds[6], part), 7)
    salvo_records = centred(part_splits[0], (CAPTURE_TALLY, SALVO_TALLY, 2, SALVO_SWEEPS, DISTANCE_BINS), 1.0, 6.0, ((0, 16),))
    stencil_weights = centred(part_splits[1], (CAPTURE_TALLY, SALVO_TALLY, STENCIL_WEIGHTS), STENCIL_WEIGHTS ** -0.5, 2.0, ((0, 16),))
    zone_drifts = touch_ends(jax.random.randint(part_splits[2], (CAPTURE_TALLY, SALVO_TALLY), 0 - BAND_DRIFT_LIMIT, BAND_DRIFT_LIMIT + 1), jax.random.fold_in(part_splits[2], 1), 0 - BAND_DRIFT_LIMIT, BAND_DRIFT_LIMIT).astype(jnp.int32)
    seam_sweeps = touch_ends(jax.random.randint(part_splits[3], (CAPTURE_TALLY, SALVO_TALLY - 1), JOINT_SWEEPS_LOW, JOINT_SWEEPS_TOP + 1), jax.random.fold_in(part_splits[3], 1), JOINT_SWEEPS_LOW, JOINT_SWEEPS_TOP).astype(jnp.int32)
    prior_sweeps = touch_ends(jax.random.randint(part_splits[4], (CAPTURE_TALLY,), 0, OFF + 1), jax.random.fold_in(part_splits[4], 1), 0, OFF).astype(jnp.int32)
    viewing_frames = draw_viewing_frames(jax.random.fold_in(jax.random.fold_in(seeds[6], part), 71), part)
    return {"salvo_records": salvo_records, "stencil_weights": stencil_weights, "zone_drifts": zone_drifts, "seam_sweeps": seam_sweeps, "prior_sweeps": prior_sweeps, "viewing_frames": viewing_frames}


EPSILON = 1e-06
SHRINK = 0.05

def regridding_tableau(tap_row, offset, distance_readings):
    rows = lax.broadcasted_iota(jnp.int32, (distance_readings, distance_readings), 0)
    downward_entry_list = lax.broadcasted_iota(jnp.int32, (distance_readings, distance_readings), 1)
    distance = rows - downward_entry_list - offset.astype(jnp.int32) + (STENCIL_WEIGHTS // 2 - 1)
    matrix = jnp.zeros((distance_readings, distance_readings), jnp.bfloat16)
    for tap_index in range(STENCIL_WEIGHTS):
        matrix = jnp.where(distance == tap_index, tap_row[tap_index], matrix)
    return matrix

def seam_lone_capture(piled_salvos, stencil_weight_table, distance_drifts, joint_sweep, opening_salvo, sweep_labels):
    distance_readings = piled_salvos.shape[-1]
    sweeps_each_salvo = piled_salvos.shape[2]
    regridding_zones = jnp.stack([regridding_tableau(stencil_weight_table[salvo_label], distance_drifts[salvo_label], distance_readings) for salvo_label in range(SALVO_TALLY)])
    regridded_salvos = jnp.einsum('bndo,bot->bndt', piled_salvos.astype(jnp.float32), regridding_zones.astype(jnp.float32)).astype(jnp.bfloat16)
    sweep_spacing = (sweeps_each_salvo - joint_sweep).astype(jnp.int32)
    salvo_beginnings = jnp.concatenate([jnp.zeros((1,), jnp.int32), jnp.cumsum(sweep_spacing).astype(jnp.int32)]) - opening_salvo.astype(jnp.int32)
    flight_sweep_slot = lax.broadcasted_iota(jnp.int32, (sweep_labels, sweeps_each_salvo), 0)
    sweep_slot = lax.broadcasted_iota(jnp.int32, (sweep_labels, sweeps_each_salvo), 1)
    downward_entry_list = []
    for salvo_label in range(SALVO_TALLY):
        seam_ramp = jnp.ones((sweep_labels, sweeps_each_salvo), jnp.float32)
        if salvo_label > 0:
            upward_ramp = (flight_sweep_slot - salvo_beginnings[salvo_label] + 1).astype(jnp.float32) / (joint_sweep[salvo_label - 1] + 1).astype(jnp.float32)
            seam_ramp = seam_ramp * jnp.clip(upward_ramp, 0.0, 1.0)
        if salvo_label < SALVO_TALLY - 1:
            downward_ramp = (salvo_beginnings[salvo_label] + sweeps_each_salvo - flight_sweep_slot).astype(jnp.float32) / (joint_sweep[salvo_label] + 1).astype(jnp.float32)
            seam_ramp = seam_ramp * jnp.clip(downward_ramp, 0.0, 1.0)
        downward_entry_list.append(jnp.where(flight_sweep_slot == salvo_beginnings[salvo_label] + sweep_slot, seam_ramp, 0.0).astype(jnp.bfloat16))
    sweep_target_slot = jnp.stack(downward_entry_list, axis=1)
    return jnp.einsum('tzg,zugi->uti', sweep_target_slot.astype(jnp.float32), regridded_salvos.astype(jnp.float32)).astype(jnp.bfloat16)

def coupling_frames(readings, native_picture_elements):
    sample_real = readings[:, 0].astype(jnp.float32)
    sample_imaginary = readings[:, 1].astype(jnp.float32)

    def pair(left, right):
        return jnp.einsum('dwm,ewm->wde', left, right)
    inverse_looks = 1.0 / LOOKS
    covariance_real = (pair(sample_real, sample_real) + pair(sample_imaginary, sample_imaginary)) * inverse_looks
    mixed = pair(sample_imaginary, sample_real)
    covariance_imaginary = (mixed - jnp.swapaxes(mixed, 1, 2)) * inverse_looks
    dates = readings.shape[0]
    inverse_root = lax.rsqrt(jnp.diagonal(covariance_real, axis1=1, axis2=2) + EPSILON)
    outer = inverse_root[:, :, None] * inverse_root[:, None, :]
    identity = jnp.eye(dates, dtype=jnp.float32)
    coherence_real = (1.0 - SHRINK) * covariance_real * outer + SHRINK * identity
    coherence_imaginary = (1.0 - SHRINK) * covariance_imaginary * outer
    vector_real = jnp.ones(inverse_root.shape, jnp.float32)
    vector_imaginary = jnp.zeros(inverse_root.shape, jnp.float32)

    def apply_matrix(matrix, vector):
        return jnp.einsum('wde,we->wd', matrix, vector, precision=lax.Precision.HIGHEST)
    for iteration in range(ITERS):
        image_real = apply_matrix(coherence_real, vector_real) - apply_matrix(coherence_imaginary, vector_imaginary)
        image_imaginary = apply_matrix(coherence_real, vector_imaginary) + apply_matrix(coherence_imaginary, vector_real)
        factor = lax.rsqrt(lax.optimization_barrier(jnp.mean(image_real * image_real + image_imaginary * image_imaginary, axis=1, keepdims=True)) + EPSILON)
        vector_real = image_real * factor
        vector_imaginary = image_imaginary * factor
    coupled_result = jnp.stack([vector_real, vector_imaginary]).astype(jnp.bfloat16)
    own_real = native_picture_elements[:, 0].astype(jnp.float32)
    own_imaginary = native_picture_elements[:, 1].astype(jnp.float32)
    history_real = coupled_result[0].astype(jnp.float32)
    history_imaginary = coupled_result[1].astype(jnp.float32)

    def project(history, pixels):
        return jnp.einsum('wd,dwm->wm', history, pixels)
    scaling = 1.0 / math.sqrt(dates)
    compressed_real = (project(history_real, own_real) + project(history_imaginary, own_imaginary)) * scaling
    compressed_imaginary = (project(history_real, own_imaginary) - project(history_imaginary, own_real)) * scaling
    condensed_result = jnp.stack([compressed_real, compressed_imaginary]).astype(jnp.bfloat16)
    return (condensed_result, coupled_result)

def dft_tables(length, span):
    first = lax.broadcasted_iota(jnp.int32, (span, span), 0)
    second = lax.broadcasted_iota(jnp.int32, (span, span), 1)
    product = first % length * (second % length) % length
    angle = product.astype(jnp.float32) * (2.0 * math.pi / length)
    inside = first // length == second // length
    cosine = jnp.where(inside, jnp.cos(angle), 0.0).astype(jnp.bfloat16)
    sine = jnp.where(inside, jnp.sin(angle), 0.0).astype(jnp.bfloat16)
    return (cosine, sine)

def goldstein(rebuilt):
    sweep_labels = rebuilt.shape[1]
    distance_readings = rebuilt.shape[2]
    range_cos, range_sin = dft_tables(PATCH, 128)
    line_cos, line_sin = dft_tables(PATCH, PATCH)

    def across(matrix, table):
        return jnp.dot(matrix.reshape(-1, 128), table, preferred_element_type=jnp.float32).reshape(sweep_labels, distance_readings)

    def along(table, matrix):
        return jnp.einsum('kn,pnr->pkr', table.astype(jnp.float32), matrix.reshape(sweep_labels // PATCH, PATCH, distance_readings).astype(jnp.float32))
    real_in = rebuilt[0]
    imaginary_in = rebuilt[1]
    first_real = (across(real_in, range_cos) + across(imaginary_in, range_sin)).astype(jnp.bfloat16)
    first_imaginary = (across(imaginary_in, range_cos) - across(real_in, range_sin)).astype(jnp.bfloat16)
    spectrum_real = along(line_cos, first_real) + along(line_sin, first_imaginary)
    spectrum_imaginary = along(line_cos, first_imaginary) - along(line_sin, first_real)
    power = spectrum_real * spectrum_real + spectrum_imaginary * spectrum_imaginary
    patch_total = lax.optimization_barrier(jnp.sum(power, axis=1)).reshape(sweep_labels // PATCH, distance_readings // PATCH, PATCH).sum(axis=2)
    patch_mean = jnp.repeat(patch_total / (PATCH * PATCH), PATCH, axis=1)[:, None, :]
    seam_ramp = jnp.sqrt(jnp.sqrt(power / (patch_mean + EPSILON)))
    weighted_real = (spectrum_real * seam_ramp).astype(jnp.bfloat16)
    weighted_imaginary = (spectrum_imaginary * seam_ramp).astype(jnp.bfloat16)
    back_real = (along(line_cos, weighted_real) - along(line_sin, weighted_imaginary)).astype(jnp.bfloat16)
    back_imaginary = (along(line_cos, weighted_imaginary) + along(line_sin, weighted_real)).astype(jnp.bfloat16)
    scaling = 1.0 / (PATCH * PATCH)
    out_real = ((across(back_real, range_cos) - across(back_imaginary, range_sin)) * scaling).astype(jnp.bfloat16)
    out_imaginary = ((across(back_imaginary, range_cos) + across(back_real, range_sin)) * scaling).astype(jnp.bfloat16)
    return jnp.stack([out_real, out_imaginary])

def reference(salvo_records, stencil_weights, zone_drifts, seam_sweeps, prior_sweeps, viewing_frames):
    seamed_picture = lax.map(lambda salvo_components: seam_lone_capture(salvo_components[0], salvo_components[1], salvo_components[2], salvo_components[3], salvo_components[4], FLIGHT_SWEEPS), (salvo_records, stencil_weights, zone_drifts, seam_sweeps, prior_sweeps))
    padded = jnp.pad(seamed_picture, ((0, 0), (0, 0), (1, 1), (0, 0)))
    flat = padded.reshape(CAPTURE_TALLY, 2, (FLIGHT_SWEEPS + 2) * DISTANCE_BINS)
    window_index = lax.broadcasted_iota(jnp.int32, (WINDOWS, LOOKS), 0)
    global_index = (window_index // WIN_DEV * (LB * DISTANCE_BINS) + viewing_frames.astype(jnp.int32)).astype(jnp.int32)
    readings = jnp.take(flat, global_index.reshape(-1), axis=2).reshape(CAPTURE_TALLY, 2, N_DATE, WIN_DEV, LOOKS)
    native_picture_elements = seamed_picture.reshape(CAPTURE_TALLY, 2, N_DATE, WIN_DEV, LOOKS)
    readings = jnp.moveaxis(readings, 2, 0)
    native_picture_elements = jnp.moveaxis(native_picture_elements, 2, 0)
    condensed_result, coupled_result = lax.map(lambda salvo_components: coupling_frames(salvo_components[0], salvo_components[1]), (readings, native_picture_elements))
    condensed_result = jnp.moveaxis(condensed_result, 0, 1).reshape(2, WINDOWS, LOOKS)
    coupled_result = jnp.moveaxis(coupled_result, 0, 1).reshape(2, WINDOWS, CAPTURE_TALLY)
    value_real = condensed_result[0].astype(jnp.float32)
    value_imaginary = condensed_result[1].astype(jnp.float32)

    def per_date(history):
        history_real = history[0].astype(jnp.float32)[:, None]
        history_imaginary = history[1].astype(jnp.float32)[:, None]
        rebuilt = jnp.stack([value_real * history_real - value_imaginary * history_imaginary, value_real * history_imaginary + value_imaginary * history_real]).astype(jnp.bfloat16)
        return goldstein(rebuilt.reshape(2, FLIGHT_SWEEPS, DISTANCE_BINS))
    return lax.map(per_date, jnp.transpose(coupled_result, (2, 0, 1)))
```

```python
import functools
import math

import jax
import jax.numpy as jnp
import ml_dtypes
import numpy as np
from jax import lax
from jax.experimental import pallas as pl
from jax.experimental.pallas import tpu as pltpu

LB = 2
TAPS = 8
LOOKS = 128
ITERS = 8
PATCH = 32
LANES = 128
EPSILON = 1e-06
SHRINK = 0.05
F32 = jnp.float32
BF16 = jnp.bfloat16


def ceil_to(value, step):
    return -(-value // step) * step


def filter_tables(chunks):
    def pair(span):
        index = np.arange(span)
        product = (index[:, None] % PATCH) * (index[None, :] % PATCH) % PATCH
        angle = product.astype(np.float32) * np.float32(2.0 * math.pi / PATCH)
        inside = index[:, None] // PATCH == index[None, :] // PATCH
        return np.where(inside, np.cos(angle), 0.0), np.where(inside, np.sin(angle), 0.0)

    cosine, sine = pair(LANES)
    line_cos, line_sin = pair(PATCH)
    eye = np.eye(chunks)
    forward = np.block([[cosine, -sine], [sine, cosine]])
    inverse = np.block([[cosine, sine], [-sine, cosine]])
    lines = np.concatenate([np.kron(line_cos, eye), np.kron(line_sin, eye)], axis=1)
    return tuple(t.astype(ml_dtypes.bfloat16) for t in (forward, lines, inverse))


def dot(a, b, **kw):
    return jnp.dot(a, b, preferred_element_type=F32, **kw)


def turned(v):
    half = v.shape[0] // 2
    return jnp.concatenate([-v[half:], v[:half]], axis=0)


def resample_and_merge(x, taps, drifts, seams, prior, lines, xp, stage, send):
    bursts, _, sweeps, cells = x.shape[1:]
    depth = xp.shape[1] // 2
    chunks = cells // LANES
    xp[...] = jnp.zeros_like(xp)
    for b in range(bursts):
        for c in range(2):
            xp[b, c * depth : c * depth + sweeps, LANES : LANES + cells] = x[0, b, c].astype(F32)
    weights = taps[0].astype(F32)
    apart = (
        lax.broadcasted_iota(jnp.int32, (3 * LANES, LANES), 0)
        - lax.broadcasted_iota(jnp.int32, (3 * LANES, LANES), 1)
        - LANES
        + (TAPS // 2 - 1)
    )
    resampled = []
    for b in range(bursts):
        distance = apart - drifts[0, b]
        band = jnp.zeros((3 * LANES, LANES), F32)
        for k in range(TAPS):
            band = jnp.where(distance == k, weights[b : b + 1, k : k + 1], band)
        left = jnp.concatenate(
            [xp[b, :, k * LANES : (k + 3) * LANES] for k in range(chunks)], axis=0
        ).astype(BF16)
        resampled.append(dot(left, band.astype(BF16)).astype(BF16))
    columns = [
        jnp.concatenate(
            [r[(k * 2 + c) * depth : (k * 2 + c + 1) * depth] for r in resampled], axis=0
        )
        for c in range(2)
        for k in range(chunks)
    ]
    rows = send.shape[0]
    line = lax.broadcasted_iota(jnp.int32, (rows, bursts * depth), 0) - 1
    sweep = lax.broadcasted_iota(jnp.int32, (rows, bursts * depth), 1)
    place = jnp.zeros((rows, bursts * depth), F32)
    start = -prior[0]
    for b in range(bursts):
        if b > 0:
            start = start + sweeps - seams[0, b - 1]
        own = sweep - b * depth
        ramp = jnp.ones((rows, bursts * depth), F32)
        if b > 0:
            shared = jnp.full((1, 1), seams[0, b - 1] + 1, jnp.int32).astype(F32)
            ramp = ramp * jnp.clip((line - start + 1).astype(F32) / shared, 0.0, 1.0)
        if b < bursts - 1:
            shared = jnp.full((1, 1), seams[0, b] + 1, jnp.int32).astype(F32)
            ramp = ramp * jnp.clip((start + sweeps - line).astype(F32) / shared, 0.0, 1.0)
        here = (line == start + own) & (own >= 0) & (own < sweeps) & (line >= 0) & (line < lines)
        place = jnp.where(here, ramp, place)
    merged = dot(place.astype(BF16), jnp.concatenate(columns, axis=1))
    width = 2 * chunks
    for j in range(width):
        stage[pl.ds(j, rows, stride=width), :] = merged[:, j * LANES : (j + 1) * LANES]
    send[...] = stage[...].astype(BF16).reshape(send.shape)


def link(dates, frames, arrived, table, table16, gram, stage, send):
    windows = frames.shape[0]
    local_lines = arrived.shape[1]
    chunks = arrived.shape[2] // 2
    both = 2 * dates
    small = dates <= 16

    def spread(d, carry):
        for l in range(local_lines):
            half, base = l // (local_lines // 2), (l % (local_lines // 2)) * chunks
            tile = arrived[d, l].astype(F32)
            for c in range(2):
                table[half, pl.ds(base * both + c * dates + d, chunks, stride=both), :] = tile[
                    c * chunks : (c + 1) * chunks
                ]
        return carry

    lax.fori_loop(0, dates, spread, 0, unroll=small)
    for half in range(2):
        table16[:, half * LANES : (half + 1) * LANES] = table[half].astype(BF16)
    groups = local_lines // 2 * chunks
    extent = groups * LANES
    cell = lax.broadcasted_iota(jnp.int32, (2 * LANES, LOOKS), 0)

    def look(w, carry):
        frame = frames[pl.ds(w, 1), :]
        high = (frame >= extent).astype(jnp.int32)
        rest = frame - high * extent
        low = (rest & (LANES - 1)) + high * LANES
        group = rest >> 7
        hot = jnp.where(cell == low, 1.0, 0.0).astype(BF16)
        if small:
            found = dot(table16[...], hot)
            z = jnp.zeros((both, LOOKS), F32)
            for g in range(groups):
                z = jnp.where(group == g, found[g * both : (g + 1) * both], z)
        else:

            def pick(g, z):
                at = pl.ds(pl.multiple_of(g * both, both), both)
                return jnp.where(group == g, dot(table16[at, :], hot), z)

            z = lax.fori_loop(0, groups, pick, jnp.zeros((both, LOOKS), F32))
        z = jnp.concatenate([z, turned(z)], axis=1).astype(BF16)
        gram[w] = lax.dot_general(z, z, (((1,), (1,)), ((), ())), preferred_element_type=F32) * (
            1.0 / LOOKS
        )
        return carry

    lax.fori_loop(0, windows, look, 0, unroll=small)
    cov = gram[...]
    shape = (1, both, both)
    eye = lax.broadcasted_iota(jnp.int32, shape, 1) == lax.broadcasted_iota(jnp.int32, shape, 2)
    diagonal = jnp.where(eye, cov, 0.0)
    root_row = lax.rsqrt(jnp.sum(diagonal, axis=1, keepdims=True) + EPSILON)
    root_col = lax.rsqrt(jnp.sum(diagonal, axis=2, keepdims=True) + EPSILON)
    gram[...] = (1.0 - SHRINK) * cov * root_col * root_row + jnp.where(eye, SHRINK, 0.0)

    def two_steps(_, v):
        for axis in (1, 2):
            u = jnp.sum(gram[...] * v, axis=axis, keepdims=True)
            norm = jnp.sum(u * u, axis=3 - axis, keepdims=True) * (1.0 / dates)
            v = u * lax.rsqrt(norm + EPSILON)
        return v

    column = lax.broadcasted_iota(jnp.int32, (windows, both, 1), 1)
    v = jnp.where(column < dates, 1.0, 0.0).astype(F32)
    v = lax.fori_loop(0, ITERS // 2, two_steps, v, unroll=small)
    linked = v.astype(BF16).astype(F32)
    for w in range(windows):
        l, k = 1 + w // chunks, w % chunks
        half, base = l // (local_lines // 2), (l % (local_lines // 2)) * chunks
        own = table[half, (base + k) * both : (base + k + 1) * both, :]
        hist = jnp.broadcast_to(linked[w], own.shape)
        turn = turned(hist)
        scale = 1.0 / math.sqrt(dates)
        real = (jnp.sum(hist * own, axis=0, keepdims=True) * scale).astype(BF16).astype(F32)
        imag = (jnp.sum(turn * own, axis=0, keepdims=True) * scale).astype(BF16).astype(F32)
        rebuilt = real * hist + imag * turn
        for c in range(2):
            stage[pl.ds(c * windows + w, dates, stride=2 * windows), :] = rebuilt[
                c * dates : (c + 1) * dates
            ]
    send[...] = stage[...].astype(BF16).reshape(send.shape)


def patch_filter(arrived, forward, lines, inverse, stage, out):
    devices, rows = arrived.shape[0], arrived.shape[1] // 2
    chunks = rows // LB
    per = PATCH // LB
    shape = (LANES, LANES)
    same = (
        lax.broadcasted_iota(jnp.int32, shape, 0) // PATCH
        == lax.broadcasted_iota(jnp.int32, shape, 1) // PATCH
    )
    ones = jnp.where(same, 1.0 / (PATCH * PATCH), 0.0).astype(F32)

    def crossed(pair, sign):
        first, second = pair[:, :LANES], pair[:, LANES:]
        flipped = [second, -first] if sign > 0 else [-second, first]
        return jnp.concatenate([pair, jnp.concatenate(flipped, axis=1)], axis=0).astype(BF16)

    for p in range(devices // per):
        block = arrived[p * per : (p + 1) * per]
        image = jnp.concatenate(
            [block[:, c * rows : (c + 1) * rows].reshape(per * rows, LANES) for c in range(2)],
            axis=1,
        )
        first = dot(image, forward[...])
        spectrum = dot(lines[...], crossed(first, 1))
        real = spectrum[:, :LANES].reshape(PATCH, chunks, LANES)
        imag = spectrum[:, LANES:].reshape(PATCH, chunks, LANES)
        power = real * real + imag * imag
        mean = dot(jnp.sum(power, axis=0), ones, precision=lax.Precision.HIGHEST)
        ramp = jnp.sqrt(jnp.sqrt(power * (1.0 / (mean + EPSILON))[None]))
        weighted = jnp.concatenate(
            [(part * ramp).reshape(per * rows, LANES) for part in (real, imag)], axis=1
        )
        back = dot(lines[...], crossed(weighted, -1)).astype(BF16)
        filtered = dot(back, inverse[...]) * (1.0 / (PATCH * PATCH))
        for c in range(2):
            stage[c] = filtered[:, c * LANES : (c + 1) * LANES]
            for k in range(chunks):
                out[0, c, p * PATCH : (p + 1) * PATCH, k * LANES : (k + 1) * LANES] = stage[
                    c, pl.ds(k, PATCH, stride=chunks), :
                ].astype(BF16)


def kernel(
    dates, x, taps, drifts, seams, prior, frames, forward, lines, inverse, out,
    xp, stage1, send1, got1, table, table16, gram, stage2, send2, got2, stage3,
    out_sem1, in_sem1, out_sem2, in_sem2,
):
    me = lax.axis_index("date")
    small = dates <= 16

    def others(body):
        def step(off, carry):
            body(off, lax.rem(me + off, dates), lax.rem(me + dates - off, dates))
            return carry

        lax.fori_loop(1, dates, step, 0, unroll=small)

    barrier = pltpu.get_barrier_semaphore()
    others(
        lambda off, to, _: pl.semaphore_signal(
            barrier, inc=1, device_id={"date": to}, device_id_type=pl.DeviceIdType.MESH
        )
    )
    resample_and_merge(x, taps, drifts, seams, prior, LB * dates, xp, stage1, send1)
    pl.semaphore_wait(barrier, dates - 1)

    def copy(source, target, off, to, landing, out_sem, in_sem):
        return pltpu.make_async_remote_copy(
            src_ref=source,
            dst_ref=target.at[landing],
            send_sem=out_sem.at[off],
            recv_sem=in_sem.at[landing],
            device_id={"date": to},
            device_id_type=pl.DeviceIdType.MESH,
        )

    def block(g):
        return send1.at[pl.ds(g * LB, LB + 2)]

    others(lambda off, to, _: copy(block(to), got1, off, to, me, out_sem1, in_sem1).start())
    got1[me] = send1[pl.ds(me * LB, LB + 2)]
    others(lambda off, to, src: copy(block(to), got1, off, to, src, out_sem1, in_sem1).wait_recv())
    link(dates, frames, got1, table, table16, gram, stage2, send2)
    others(lambda off, to, _: copy(send2.at[to], got2, off, to, me, out_sem2, in_sem2).start())
    got2[me] = send2[me]
    others(
        lambda off, to, src: copy(send2.at[to], got2, off, to, src, out_sem2, in_sem2).wait_recv()
    )
    patch_filter(got2, forward, lines, inverse, stage3, out)
    others(lambda off, to, _: copy(block(to), got1, off, to, me, out_sem1, in_sem1).wait_send())
    others(lambda off, to, _: copy(send2.at[to], got2, off, to, me, out_sem2, in_sem2).wait_send())


def on_device(records, taps, drifts, seams, prior, frames):
    dates = lax.axis_size("date")
    _, bursts, _, sweeps, cells = records.shape
    windows = frames.shape[0]
    chunks = cells // LANES
    lines = LB * dates
    rows = ceil_to(lines + 2, 8)
    depth = ceil_to(sweeps, 16)
    width = 2 * chunks
    both = 2 * dates
    groups = (LB + 2) // 2 * chunks
    vmem = pl.BlockSpec(memory_space=pltpu.VMEM)
    smem = pl.BlockSpec(memory_space=pltpu.SMEM)
    tables = [jnp.asarray(t) for t in filter_tables(chunks)]
    return pl.pallas_call(
        functools.partial(kernel, dates),
        out_shape=jax.ShapeDtypeStruct((1, 2, lines, cells), BF16),
        in_specs=[vmem, vmem, smem, smem, smem, vmem, vmem, vmem, vmem],
        out_specs=vmem,
        scratch_shapes=[
            pltpu.VMEM((bursts, 2 * depth, cells + 2 * LANES), F32),
            pltpu.VMEM((rows * width, LANES), F32),
            pltpu.VMEM((rows, width, LANES), BF16),
            pltpu.VMEM((dates, LB + 2, width, LANES), BF16),
            pltpu.VMEM((2, groups * both, LANES), F32),
            pltpu.VMEM((groups * both, 2 * LANES), BF16),
            pltpu.VMEM((windows, both, both), F32),
            pltpu.VMEM((both * windows, LANES), F32),
            pltpu.VMEM((dates, 2 * windows, LANES), BF16),
            pltpu.VMEM((dates, 2 * windows, LANES), BF16),
            pltpu.VMEM((2, PATCH * chunks, LANES), F32),
            pltpu.SemaphoreType.DMA((dates,)),
            pltpu.SemaphoreType.DMA((dates,)),
            pltpu.SemaphoreType.DMA((dates,)),
            pltpu.SemaphoreType.DMA((dates,)),
        ],
        compiler_params=pltpu.CompilerParams(
            collective_id=0, has_side_effects=True, vmem_limit_bytes=48 * 2**20
        ),
    )(records, taps, drifts, seams, prior, frames, *tables)


def solution(mesh):
    from jax.sharding import PartitionSpec as P

    both = ("group", "date")
    return jax.shard_map(
        on_device,
        mesh=mesh,
        in_specs=(
            P(both, None, None, None, None),
            P(both, None, None),
            P(both, None),
            P(both, None),
            P(both),
            P(both, None),
        ),
        out_specs=P(both, None, None, None),
        check_vma=False,
    )
```

```python
import functools
import math

import jax
import jax.numpy as jnp
import ml_dtypes
import numpy as np
from jax import lax
from jax.experimental import pallas as pl
from jax.experimental.pallas import tpu as pltpu

LB = 2
TAPS = 8
LOOKS = 128
ITERS = 8
PATCH = 32
LANES = 128
EPSILON = 1e-06
SHRINK = 0.05
F32 = jnp.float32
BF16 = jnp.bfloat16


def ceil_to(value, step):
    return -(-value // step) * step


def filter_tables(chunks):
    def pair(span):
        index = np.arange(span)
        product = (index[:, None] % PATCH) * (index[None, :] % PATCH) % PATCH
        angle = product.astype(np.float32) * np.float32(2.0 * math.pi / PATCH)
        inside = index[:, None] // PATCH == index[None, :] // PATCH
        return np.where(inside, np.cos(angle), 0.0), np.where(inside, np.sin(angle), 0.0)

    cosine, sine = pair(LANES)
    line_cos, line_sin = pair(PATCH)
    eye = np.eye(chunks)
    forward = np.block([[cosine, -sine], [sine, cosine]])
    inverse = np.block([[cosine, sine], [-sine, cosine]])
    lines = np.concatenate([np.kron(line_cos, eye), np.kron(line_sin, eye)], axis=1)
    return tuple(t.astype(ml_dtypes.bfloat16) for t in (forward, lines, inverse))


def dot(a, b, **kw):
    return jnp.dot(a, b, preferred_element_type=F32, **kw)


def turned(v):
    half = v.shape[0] // 2
    return jnp.concatenate([-v[half:], v[:half]], axis=0)


def resample_and_merge(x, taps, drifts, seams, prior, lines, xp, stage, send):
    bursts, sweeps, _, cells = x.shape[1:]
    depth = xp.shape[1] // 2
    chunks = cells // LANES
    xp[...] = jnp.zeros_like(xp)
    for b in range(bursts):
        for c in range(2):
            xp[b, c * depth : c * depth + sweeps, LANES : LANES + cells] = x[0, b, :, c, :].astype(F32)
    weights = taps[0].astype(F32)
    apart = (
        lax.broadcasted_iota(jnp.int32, (3 * LANES, LANES), 0)
        - lax.broadcasted_iota(jnp.int32, (3 * LANES, LANES), 1)
        - LANES
        + (TAPS // 2 - 1)
    )
    resampled = []
    for b in range(bursts):
        distance = apart - drifts[0, b]
        band = jnp.zeros((3 * LANES, LANES), F32)
        for k in range(TAPS):
            band = jnp.where(distance == k, weights[b : b + 1, k : k + 1], band)
        left = jnp.concatenate(
            [xp[b, :, k * LANES : (k + 3) * LANES] for k in range(chunks)], axis=0
        ).astype(BF16)
        resampled.append(dot(left, band.astype(BF16)).astype(BF16))
    columns = [
        jnp.concatenate(
            [r[(k * 2 + c) * depth : (k * 2 + c + 1) * depth] for r in resampled], axis=0
        )
        for c in range(2)
        for k in range(chunks)
    ]
    rows = send.shape[0]
    line = lax.broadcasted_iota(jnp.int32, (rows, bursts * depth), 0) - 1
    sweep = lax.broadcasted_iota(jnp.int32, (rows, bursts * depth), 1)
    place = jnp.zeros((rows, bursts * depth), F32)
    start = -prior[0]
    for b in range(bursts):
        if b > 0:
            start = start + sweeps - seams[0, b - 1]
        own = sweep - b * depth
        ramp = jnp.ones((rows, bursts * depth), F32)
        if b > 0:
            shared = jnp.full((1, 1), seams[0, b - 1] + 1, jnp.int32).astype(F32)
            ramp = ramp * jnp.clip((line - start + 1).astype(F32) / shared, 0.0, 1.0)
        if b < bursts - 1:
            shared = jnp.full((1, 1), seams[0, b] + 1, jnp.int32).astype(F32)
            ramp = ramp * jnp.clip((start + sweeps - line).astype(F32) / shared, 0.0, 1.0)
        here = (line == start + own) & (own >= 0) & (own < sweeps) & (line >= 0) & (line < lines)
        place = jnp.where(here, ramp, place)
    merged = dot(place.astype(BF16), jnp.concatenate(columns, axis=1))
    width = 2 * chunks
    for j in range(width):
        stage[pl.ds(j, rows, stride=width), :] = merged[:, j * LANES : (j + 1) * LANES]
    send[...] = stage[...].astype(BF16).reshape(send.shape)


def link(dates, frames, arrived, table, table16, gram, stage, send):
    windows = frames.shape[0]
    local_lines = arrived.shape[1]
    chunks = arrived.shape[2] // 2
    both = 2 * dates
    small = dates <= 16

    def spread(d, carry):
        for l in range(local_lines):
            half, base = l // (local_lines // 2), (l % (local_lines // 2)) * chunks
            tile = arrived[d, l].astype(F32)
            for c in range(2):
                table[half, pl.ds(base * both + c * dates + d, chunks, stride=both), :] = tile[
                    c * chunks : (c + 1) * chunks
                ]
        return carry

    lax.fori_loop(0, dates, spread, 0, unroll=small)
    for half in range(2):
        table16[:, half * LANES : (half + 1) * LANES] = table[half].astype(BF16)
    groups = local_lines // 2 * chunks
    extent = groups * LANES
    cell = lax.broadcasted_iota(jnp.int32, (2 * LANES, LOOKS), 0)

    def look(w, carry):
        frame = frames[pl.ds(w, 1), :]
        high = (frame >= extent).astype(jnp.int32)
        rest = frame - high * extent
        low = (rest & (LANES - 1)) + high * LANES
        group = rest >> 7
        hot = jnp.where(cell == low, 1.0, 0.0).astype(BF16)
        if small:
            found = dot(table16[...], hot)
            z = jnp.zeros((both, LOOKS), F32)
            for g in range(groups):
                z = jnp.where(group == g, found[g * both : (g + 1) * both], z)
        else:

            def pick(g, z):
                at = pl.ds(pl.multiple_of(g * both, both), both)
                return jnp.where(group == g, dot(table16[at, :], hot), z)

            z = lax.fori_loop(0, groups, pick, jnp.zeros((both, LOOKS), F32))
        z = jnp.concatenate([z, turned(z)], axis=1).astype(BF16)
        gram[w] = lax.dot_general(z, z, (((1,), (1,)), ((), ())), preferred_element_type=F32) * (
            1.0 / LOOKS
        )
        return carry

    lax.fori_loop(0, windows, look, 0, unroll=small)
    cov = gram[...]
    shape = (1, both, both)
    eye = lax.broadcasted_iota(jnp.int32, shape, 1) == lax.broadcasted_iota(jnp.int32, shape, 2)
    diagonal = jnp.where(eye, cov, 0.0)
    root_row = lax.rsqrt(jnp.sum(diagonal, axis=1, keepdims=True) + EPSILON)
    root_col = lax.rsqrt(jnp.sum(diagonal, axis=2, keepdims=True) + EPSILON)
    gram[...] = (1.0 - SHRINK) * cov * root_col * root_row + jnp.where(eye, SHRINK, 0.0)

    def two_steps(_, v):
        for axis in (1, 2):
            u = jnp.sum(gram[...] * v, axis=axis, keepdims=True)
            norm = jnp.sum(u * u, axis=3 - axis, keepdims=True) * (1.0 / dates)
            v = u * lax.rsqrt(norm + EPSILON)
        return v

    column = lax.broadcasted_iota(jnp.int32, (windows, both, 1), 1)
    v = jnp.where(column < dates, 1.0, 0.0).astype(F32)
    v = lax.fori_loop(0, ITERS // 2, two_steps, v, unroll=small)
    linked = v.astype(BF16).astype(F32)
    for w in range(windows):
        l, k = 1 + w // chunks, w % chunks
        half, base = l // (local_lines // 2), (l % (local_lines // 2)) * chunks
        own = table[half, (base + k) * both : (base + k + 1) * both, :]
        hist = jnp.broadcast_to(linked[w], own.shape)
        turn = turned(hist)
        scale = 1.0 / math.sqrt(dates)
        real = (jnp.sum(hist * own, axis=0, keepdims=True) * scale).astype(BF16).astype(F32)
        imag = (jnp.sum(turn * own, axis=0, keepdims=True) * scale).astype(BF16).astype(F32)
        rebuilt = real * hist + imag * turn
        for c in range(2):
            stage[pl.ds(c * windows + w, dates, stride=2 * windows), :] = rebuilt[
                c * dates : (c + 1) * dates
            ]
    send[...] = stage[...].astype(BF16).reshape(send.shape)


def patch_filter(arrived, forward, lines, inverse, stage, out):
    devices, rows = arrived.shape[0], arrived.shape[1] // 2
    chunks = rows // LB
    per = PATCH // LB
    shape = (LANES, LANES)
    same = (
        lax.broadcasted_iota(jnp.int32, shape, 0) // PATCH
        == lax.broadcasted_iota(jnp.int32, shape, 1) // PATCH
    )
    ones = jnp.where(same, 1.0 / (PATCH * PATCH), 0.0).astype(F32)

    def crossed(pair, sign):
        first, second = pair[:, :LANES], pair[:, LANES:]
        flipped = [second, -first] if sign > 0 else [-second, first]
        return jnp.concatenate([pair, jnp.concatenate(flipped, axis=1)], axis=0).astype(BF16)

    for p in range(devices // per):
        block = arrived[p * per : (p + 1) * per]
        image = jnp.concatenate(
            [block[:, c * rows : (c + 1) * rows].reshape(per * rows, LANES) for c in range(2)],
            axis=1,
        )
        first = dot(image, forward[...])
        spectrum = dot(lines[...], crossed(first, 1))
        real = spectrum[:, :LANES].reshape(PATCH, chunks, LANES)
        imag = spectrum[:, LANES:].reshape(PATCH, chunks, LANES)
        power = real * real + imag * imag
        mean = dot(jnp.sum(power, axis=0), ones, precision=lax.Precision.HIGHEST)
        ramp = jnp.sqrt(jnp.sqrt(power * (1.0 / (mean + EPSILON))[None]))
        weighted = jnp.concatenate(
            [(part * ramp).reshape(per * rows, LANES) for part in (real, imag)], axis=1
        )
        back = dot(lines[...], crossed(weighted, -1)).astype(BF16)
        filtered = dot(back, inverse[...]) * (1.0 / (PATCH * PATCH))
        for c in range(2):
            stage[c] = filtered[:, c * LANES : (c + 1) * LANES]
            for k in range(chunks):
                out[0, c, p * PATCH : (p + 1) * PATCH, k * LANES : (k + 1) * LANES] = stage[
                    c, pl.ds(k, PATCH, stride=chunks), :
                ].astype(BF16)


def kernel(
    dates, x, taps, drifts, seams, prior, frames, forward, lines, inverse, out,
    xp, stage1, send1, got1, table, table16, gram, stage2, send2, got2, stage3,
    out_sem1, in_sem1, out_sem2, in_sem2, held_forward, held_lines, held_inverse, table_sem,
):
    me = lax.axis_index("date")
    held = (held_forward, held_lines, held_inverse)
    fetches = [
        pltpu.make_async_copy(source, target, table_sem.at[i])
        for i, (source, target) in enumerate(zip((forward, lines, inverse), held))
    ]
    for fetch in fetches:
        fetch.start()
    small = dates <= 16

    def others(body):
        def step(off, carry):
            body(off, lax.rem(me + off, dates), lax.rem(me + dates - off, dates))
            return carry

        lax.fori_loop(1, dates, step, 0, unroll=small)

    barrier = pltpu.get_barrier_semaphore()
    others(
        lambda off, to, _: pl.semaphore_signal(
            barrier, inc=1, device_id={"date": to}, device_id_type=pl.DeviceIdType.MESH
        )
    )
    resample_and_merge(x, taps, drifts, seams, prior, LB * dates, xp, stage1, send1)
    pl.semaphore_wait(barrier, dates - 1)

    def copy(source, target, off, to, landing, out_sem, in_sem):
        return pltpu.make_async_remote_copy(
            src_ref=source,
            dst_ref=target.at[landing],
            send_sem=out_sem.at[off],
            recv_sem=in_sem.at[landing],
            device_id={"date": to},
            device_id_type=pl.DeviceIdType.MESH,
        )

    def block(g):
        return send1.at[pl.ds(g * LB, LB + 2)]

    others(lambda off, to, _: copy(block(to), got1, off, to, me, out_sem1, in_sem1).start())
    got1[me] = send1[pl.ds(me * LB, LB + 2)]
    others(lambda off, to, src: copy(block(to), got1, off, to, src, out_sem1, in_sem1).wait_recv())
    link(dates, frames, got1, table, table16, gram, stage2, send2)
    others(lambda off, to, _: copy(send2.at[to], got2, off, to, me, out_sem2, in_sem2).start())
    got2[me] = send2[me]
    others(
        lambda off, to, src: copy(send2.at[to], got2, off, to, src, out_sem2, in_sem2).wait_recv()
    )
    for fetch in fetches:
        fetch.wait()
    patch_filter(got2, *held, stage3, out)
    others(lambda off, to, _: copy(block(to), got1, off, to, me, out_sem1, in_sem1).wait_send())
    others(lambda off, to, _: copy(send2.at[to], got2, off, to, me, out_sem2, in_sem2).wait_send())


def on_device(records, taps, drifts, seams, prior, frames):
    dates = lax.axis_size("date")
    _, bursts, _, sweeps, cells = records.shape
    windows = frames.shape[0]
    chunks = cells // LANES
    lines = LB * dates
    rows = ceil_to(lines + 2, 8)
    depth = ceil_to(sweeps, 16)
    width = 2 * chunks
    both = 2 * dates
    groups = (LB + 2) // 2 * chunks
    vmem = pl.BlockSpec(memory_space=pltpu.VMEM)
    smem = pl.BlockSpec(memory_space=pltpu.SMEM)
    far = pl.BlockSpec(memory_space=pltpu.HBM)
    tables = [jnp.asarray(t) for t in filter_tables(chunks)]
    return pl.pallas_call(
        functools.partial(kernel, dates),
        out_shape=jax.ShapeDtypeStruct((1, 2, lines, cells), BF16),
        in_specs=[vmem, vmem, smem, smem, smem, vmem, far, far, far],
        out_specs=vmem,
        scratch_shapes=[
            pltpu.VMEM((bursts, 2 * depth, cells + 2 * LANES), F32),
            pltpu.VMEM((rows * width, LANES), F32),
            pltpu.VMEM((rows, width, LANES), BF16),
            pltpu.VMEM((dates, LB + 2, width, LANES), BF16),
            pltpu.VMEM((2, groups * both, LANES), F32),
            pltpu.VMEM((groups * both, 2 * LANES), BF16),
            pltpu.VMEM((windows, both, both), F32),
            pltpu.VMEM((both * windows, LANES), F32),
            pltpu.VMEM((dates, 2 * windows, LANES), BF16),
            pltpu.VMEM((dates, 2 * windows, LANES), BF16),
            pltpu.VMEM((2, PATCH * chunks, LANES), F32),
            pltpu.SemaphoreType.DMA((dates,)),
            pltpu.SemaphoreType.DMA((dates,)),
            pltpu.SemaphoreType.DMA((dates,)),
            pltpu.SemaphoreType.DMA((dates,)),
            *[pltpu.VMEM(t.shape, BF16) for t in tables],
            pltpu.SemaphoreType.DMA((len(tables),)),
        ],
        compiler_params=pltpu.CompilerParams(
            collective_id=0, has_side_effects=True, vmem_limit_bytes=60 * 2**20
        ),
    )(jnp.swapaxes(records, 2, 3), taps, drifts, seams, prior, frames, *tables)


def solution(mesh):
    from jax.sharding import PartitionSpec as P

    both = ("group", "date")
    return jax.shard_map(
        on_device,
        mesh=mesh,
        in_specs=(
            P(both, None, None, None, None),
            P(both, None, None),
            P(both, None),
            P(both, None),
            P(both),
            P(both, None),
        ),
        out_specs=P(both, None, None, None),
        check_vma=False,
    )
```

```python
import functools
import math

import jax
import jax.numpy as jnp
import ml_dtypes
import numpy as np
from jax import lax
from jax.experimental import pallas as pl
from jax.experimental.pallas import tpu as pltpu

LB = 2
TAPS = 8
LOOKS = 128
ITERS = 8
PATCH = 32
LANES = 128
EPSILON = 1e-06
SHRINK = 0.05
F32 = jnp.float32
BF16 = jnp.bfloat16


def ceil_to(value, step):
    return -(-value // step) * step


def filter_tables(chunks):
    def pair(span):
        index = np.arange(span)
        product = (index[:, None] % PATCH) * (index[None, :] % PATCH) % PATCH
        angle = product.astype(np.float32) * np.float32(2.0 * math.pi / PATCH)
        inside = index[:, None] // PATCH == index[None, :] // PATCH
        return np.where(inside, np.cos(angle), 0.0), np.where(inside, np.sin(angle), 0.0)

    cosine, sine = pair(LANES)
    line_cos, line_sin = pair(PATCH)
    eye = np.eye(chunks)
    forward = np.block([[cosine, -sine], [sine, cosine]])
    inverse = np.block([[cosine, sine], [-sine, cosine]])
    lines = np.concatenate([np.kron(line_cos, eye), np.kron(line_sin, eye)], axis=1)
    return tuple(t.astype(ml_dtypes.bfloat16) for t in (forward, lines, inverse))


def dot(a, b, **kw):
    return jnp.dot(a, b, preferred_element_type=F32, **kw)


def turned(v):
    half = v.shape[0] // 2
    return jnp.concatenate([-v[half:], v[:half]], axis=0)


def resample_and_merge(x, taps, drifts, seams, prior, lines, xp, stage, send):
    bursts, sweeps, _, cells = x.shape[1:]
    depth = xp.shape[1] // 2
    chunks = cells // LANES
    xp[...] = jnp.zeros_like(xp)
    for b in range(bursts):
        for c in range(2):
            xp[b, c * depth : c * depth + sweeps, LANES : LANES + cells] = x[0, b, :, c, :].astype(F32)
    weights = taps[0].astype(F32)
    apart = (
        lax.broadcasted_iota(jnp.int32, (3 * LANES, LANES), 0)
        - lax.broadcasted_iota(jnp.int32, (3 * LANES, LANES), 1)
        - LANES
        + (TAPS // 2 - 1)
    )
    resampled = []
    for b in range(bursts):
        distance = apart - drifts[0, b]
        band = jnp.zeros((3 * LANES, LANES), F32)
        for k in range(TAPS):
            band = jnp.where(distance == k, weights[b : b + 1, k : k + 1], band)
        left = jnp.concatenate(
            [xp[b, :, k * LANES : (k + 3) * LANES] for k in range(chunks)], axis=0
        ).astype(BF16)
        resampled.append(dot(left, band.astype(BF16)).astype(BF16))
    columns = [
        jnp.concatenate(
            [r[(k * 2 + c) * depth : (k * 2 + c + 1) * depth] for r in resampled], axis=0
        )
        for c in range(2)
        for k in range(chunks)
    ]
    rows = send.shape[0]
    line = lax.broadcasted_iota(jnp.int32, (rows, bursts * depth), 0) - 1
    sweep = lax.broadcasted_iota(jnp.int32, (rows, bursts * depth), 1)
    place = jnp.zeros((rows, bursts * depth), F32)
    start = -prior[0]
    for b in range(bursts):
        if b > 0:
            start = start + sweeps - seams[0, b - 1]
        own = sweep - b * depth
        ramp = jnp.ones((rows, bursts * depth), F32)
        if b > 0:
            shared = jnp.full((1, 1), seams[0, b - 1] + 1, jnp.int32).astype(F32)
            ramp = ramp * jnp.clip((line - start + 1).astype(F32) / shared, 0.0, 1.0)
        if b < bursts - 1:
            shared = jnp.full((1, 1), seams[0, b] + 1, jnp.int32).astype(F32)
            ramp = ramp * jnp.clip((start + sweeps - line).astype(F32) / shared, 0.0, 1.0)
        here = (line == start + own) & (own >= 0) & (own < sweeps) & (line >= 0) & (line < lines)
        place = jnp.where(here, ramp, place)
    merged = dot(place.astype(BF16), jnp.concatenate(columns, axis=1))
    width = 2 * chunks
    for j in range(width):
        stage[pl.ds(j, rows, stride=width), :] = merged[:, j * LANES : (j + 1) * LANES]
    send[...] = stage[...].astype(BF16).reshape(send.shape)


def link(dates, frames, arrived, border, table, table16, gram, stage, send):
    windows = frames.shape[0]
    local_lines = arrived.shape[1]
    chunks = arrived.shape[2] // 2
    both = 2 * dates
    small = dates <= 16

    def spread(which, d, carry):
        for l in which:
            half, base = l // (local_lines // 2), (l % (local_lines // 2)) * chunks
            tile = arrived[d, l].astype(F32)
            for c in range(2):
                table[half, pl.ds(base * both + c * dates + d, chunks, stride=both), :] = tile[
                    c * chunks : (c + 1) * chunks
                ]
        return carry

    inner = functools.partial(spread, range(1, local_lines - 1))
    outer = functools.partial(spread, (0, local_lines - 1))
    lax.fori_loop(0, dates, inner, 0, unroll=small)
    border()
    lax.fori_loop(0, dates, outer, 0, unroll=small)
    for half in range(2):
        table16[:, half * LANES : (half + 1) * LANES] = table[half].astype(BF16)
    groups = local_lines // 2 * chunks
    extent = groups * LANES
    cell = lax.broadcasted_iota(jnp.int32, (2 * LANES, LOOKS), 0)

    def look(w, carry):
        frame = frames[pl.ds(w, 1), :]
        high = (frame >= extent).astype(jnp.int32)
        rest = frame - high * extent
        low = (rest & (LANES - 1)) + high * LANES
        group = rest >> 7
        hot = jnp.where(cell == low, 1.0, 0.0).astype(BF16)
        if small:
            found = dot(table16[...], hot)
            z = jnp.zeros((both, LOOKS), F32)
            for g in range(groups):
                z = jnp.where(group == g, found[g * both : (g + 1) * both], z)
        else:

            def pick(g, z):
                at = pl.ds(pl.multiple_of(g * both, both), both)
                return jnp.where(group == g, dot(table16[at, :], hot), z)

            z = lax.fori_loop(0, groups, pick, jnp.zeros((both, LOOKS), F32))
        z = jnp.concatenate([z, turned(z)], axis=1).astype(BF16)
        gram[w] = lax.dot_general(z, z, (((1,), (1,)), ((), ())), preferred_element_type=F32) * (
            1.0 / LOOKS
        )
        return carry

    lax.fori_loop(0, windows, look, 0, unroll=small)
    cov = gram[...]
    shape = (1, both, both)
    eye = lax.broadcasted_iota(jnp.int32, shape, 1) == lax.broadcasted_iota(jnp.int32, shape, 2)
    diagonal = jnp.where(eye, cov, 0.0)
    root_row = lax.rsqrt(jnp.sum(diagonal, axis=1, keepdims=True) + EPSILON)
    root_col = lax.rsqrt(jnp.sum(diagonal, axis=2, keepdims=True) + EPSILON)
    gram[...] = (1.0 - SHRINK) * cov * root_col * root_row + jnp.where(eye, SHRINK, 0.0)

    def two_steps(_, v):
        for axis in (1, 2):
            u = jnp.sum(gram[...] * v, axis=axis, keepdims=True)
            norm = jnp.sum(u * u, axis=3 - axis, keepdims=True) * (1.0 / dates)
            v = u * lax.rsqrt(norm + EPSILON)
        return v

    column = lax.broadcasted_iota(jnp.int32, (windows, both, 1), 1)
    v = jnp.where(column < dates, 1.0, 0.0).astype(F32)
    v = lax.fori_loop(0, ITERS // 2, two_steps, v, unroll=small)
    linked = v.astype(BF16).astype(F32)
    for w in range(windows):
        l, k = 1 + w // chunks, w % chunks
        half, base = l // (local_lines // 2), (l % (local_lines // 2)) * chunks
        own = table[half, (base + k) * both : (base + k + 1) * both, :]
        hist = jnp.broadcast_to(linked[w], own.shape)
        turn = turned(hist)
        scale = 1.0 / math.sqrt(dates)
        real = (jnp.sum(hist * own, axis=0, keepdims=True) * scale).astype(BF16).astype(F32)
        imag = (jnp.sum(turn * own, axis=0, keepdims=True) * scale).astype(BF16).astype(F32)
        rebuilt = real * hist + imag * turn
        for c in range(2):
            stage[pl.ds(c * windows + w, dates, stride=2 * windows), :] = rebuilt[
                c * dates : (c + 1) * dates
            ]
    send[...] = stage[...].astype(BF16).reshape(send.shape)


def patch_filter(arrived, forward, lines, inverse, stage, out):
    devices, rows = arrived.shape[0], arrived.shape[1] // 2
    chunks = rows // LB
    per = PATCH // LB
    shape = (LANES, LANES)
    same = (
        lax.broadcasted_iota(jnp.int32, shape, 0) // PATCH
        == lax.broadcasted_iota(jnp.int32, shape, 1) // PATCH
    )
    ones = jnp.where(same, 1.0 / (PATCH * PATCH), 0.0).astype(F32)

    def crossed(pair, sign):
        first, second = pair[:, :LANES], pair[:, LANES:]
        flipped = [second, -first] if sign > 0 else [-second, first]
        return jnp.concatenate([pair, jnp.concatenate(flipped, axis=1)], axis=0).astype(BF16)

    for p in range(devices // per):
        block = arrived[p * per : (p + 1) * per]
        image = jnp.concatenate(
            [block[:, c * rows : (c + 1) * rows].reshape(per * rows, LANES) for c in range(2)],
            axis=1,
        )
        first = dot(image, forward[...])
        spectrum = dot(lines[...], crossed(first, 1))
        real = spectrum[:, :LANES].reshape(PATCH, chunks, LANES)
        imag = spectrum[:, LANES:].reshape(PATCH, chunks, LANES)
        power = real * real + imag * imag
        mean = dot(jnp.sum(power, axis=0), ones, precision=lax.Precision.HIGHEST)
        ramp = jnp.sqrt(jnp.sqrt(power * (1.0 / (mean + EPSILON))[None]))
        weighted = jnp.concatenate(
            [(part * ramp).reshape(per * rows, LANES) for part in (real, imag)], axis=1
        )
        back = dot(lines[...], crossed(weighted, -1)).astype(BF16)
        filtered = dot(back, inverse[...]) * (1.0 / (PATCH * PATCH))
        for c in range(2):
            stage[c] = filtered[:, c * LANES : (c + 1) * LANES]
            for k in range(chunks):
                out[0, c, p * PATCH : (p + 1) * PATCH, k * LANES : (k + 1) * LANES] = stage[
                    c, pl.ds(k, PATCH, stride=chunks), :
                ].astype(BF16)


def kernel(
    dates, x, taps, drifts, seams, prior, frames, forward, lines, inverse, out,
    xp, stage1, send1, got1, table, table16, gram, stage2, send2, got2, stage3,
    out_sem1, in_sem1, out_sem2, in_sem2, held_forward, held_lines, held_inverse, table_sem,
    edge_out, edge_in,
):
    me = lax.axis_index("date")
    held = (held_forward, held_lines, held_inverse)
    fetches = [
        pltpu.make_async_copy(source, target, table_sem.at[i])
        for i, (source, target) in enumerate(zip((forward, lines, inverse), held))
    ]
    for fetch in fetches:
        fetch.start()
    small = dates <= 16

    def others(body):
        def step(off, carry):
            body(off, lax.rem(me + off, dates), lax.rem(me + dates - off, dates))
            return carry

        lax.fori_loop(1, dates, step, 0, unroll=small)

    barrier = pltpu.get_barrier_semaphore()
    others(
        lambda off, to, _: pl.semaphore_signal(
            barrier, inc=1, device_id={"date": to}, device_id_type=pl.DeviceIdType.MESH
        )
    )
    resample_and_merge(x, taps, drifts, seams, prior, LB * dates, xp, stage1, send1)
    pl.semaphore_wait(barrier, dates - 1)

    def landed(target, at):
        return target.at[at, pl.ds(1, LB)] if target is got1 else target.at[at]

    def copy(source, target, off, to, landing, out_sem, in_sem):
        return pltpu.make_async_remote_copy(
            src_ref=source,
            dst_ref=landed(target, landing),
            send_sem=out_sem.at[off],
            recv_sem=in_sem.at[landing],
            device_id={"date": to},
            device_id_type=pl.DeviceIdType.MESH,
        )

    def block(g):
        return send1.at[pl.ds(g * LB + 1, LB)]

    others(lambda off, to, _: copy(block(to), got1, off, to, me, out_sem1, in_sem1).start())
    got1[me, 1 : LB + 1] = send1[pl.ds(me * LB + 1, LB)]
    others(lambda off, to, src: copy(block(to), got1, off, to, src, out_sem1, in_sem1).wait_recv())

    def edge(way):
        line, landing = (LB, 0) if way else (1, LB + 1)
        to = me + 1 if way else me - 1
        return pltpu.make_async_remote_copy(
            src_ref=got1.at[:, pl.ds(line, 1)],
            dst_ref=got1.at[:, pl.ds(landing, 1)],
            send_sem=edge_out.at[way],
            recv_sem=edge_in.at[way],
            device_id={"date": to},
            device_id_type=pl.DeviceIdType.MESH,
        )

    first, last = me == 0, me == dates - 1
    pl.when(jnp.logical_not(last))(lambda: edge(1).start())
    pl.when(jnp.logical_not(first))(lambda: edge(0).start())

    def blank(line):
        got1[:, line : line + 1] = jnp.zeros((dates, 1, *got1.shape[2:]), BF16)

    def border():
        pl.when(first)(lambda: blank(0))
        pl.when(last)(lambda: blank(LB + 1))
        pl.when(jnp.logical_not(first))(lambda: edge(1).wait_recv())
        pl.when(jnp.logical_not(last))(lambda: edge(0).wait_recv())

    link(dates, frames, got1, border, table, table16, gram, stage2, send2)
    others(lambda off, to, _: copy(send2.at[to], got2, off, to, me, out_sem2, in_sem2).start())
    got2[me] = send2[me]
    others(
        lambda off, to, src: copy(send2.at[to], got2, off, to, src, out_sem2, in_sem2).wait_recv()
    )
    for fetch in fetches:
        fetch.wait()
    patch_filter(got2, *held, stage3, out)
    others(lambda off, to, _: copy(block(to), got1, off, to, me, out_sem1, in_sem1).wait_send())
    pl.when(jnp.logical_not(last))(lambda: edge(1).wait_send())
    pl.when(jnp.logical_not(first))(lambda: edge(0).wait_send())
    others(lambda off, to, _: copy(send2.at[to], got2, off, to, me, out_sem2, in_sem2).wait_send())


def on_device(records, taps, drifts, seams, prior, frames):
    dates = lax.axis_size("date")
    _, bursts, _, sweeps, cells = records.shape
    windows = frames.shape[0]
    chunks = cells // LANES
    lines = LB * dates
    rows = ceil_to(lines + 2, 8)
    depth = ceil_to(sweeps, 16)
    width = 2 * chunks
    both = 2 * dates
    groups = (LB + 2) // 2 * chunks
    vmem = pl.BlockSpec(memory_space=pltpu.VMEM)
    smem = pl.BlockSpec(memory_space=pltpu.SMEM)
    far = pl.BlockSpec(memory_space=pltpu.HBM)
    tables = [jnp.asarray(t) for t in filter_tables(chunks)]
    return pl.pallas_call(
        functools.partial(kernel, dates),
        out_shape=jax.ShapeDtypeStruct((1, 2, lines, cells), BF16),
        in_specs=[vmem, vmem, smem, smem, smem, vmem, far, far, far],
        out_specs=vmem,
        scratch_shapes=[
            pltpu.VMEM((bursts, 2 * depth, cells + 2 * LANES), F32),
            pltpu.VMEM((rows * width, LANES), F32),
            pltpu.VMEM((rows, width, LANES), BF16),
            pltpu.VMEM((dates, LB + 2, width, LANES), BF16),
            pltpu.VMEM((2, groups * both, LANES), F32),
            pltpu.VMEM((groups * both, 2 * LANES), BF16),
            pltpu.VMEM((windows, both, both), F32),
            pltpu.VMEM((both * windows, LANES), F32),
            pltpu.VMEM((dates, 2 * windows, LANES), BF16),
            pltpu.VMEM((dates, 2 * windows, LANES), BF16),
            pltpu.VMEM((2, PATCH * chunks, LANES), F32),
            pltpu.SemaphoreType.DMA((dates,)),
            pltpu.SemaphoreType.DMA((dates,)),
            pltpu.SemaphoreType.DMA((dates,)),
            pltpu.SemaphoreType.DMA((dates,)),
            *[pltpu.VMEM(t.shape, BF16) for t in tables],
            pltpu.SemaphoreType.DMA((len(tables),)),
            pltpu.SemaphoreType.DMA((2,)),
            pltpu.SemaphoreType.DMA((2,)),
        ],
        compiler_params=pltpu.CompilerParams(
            collective_id=0, has_side_effects=True, vmem_limit_bytes=60 * 2**20
        ),
    )(jnp.swapaxes(records, 2, 3), taps, drifts, seams, prior, frames, *tables)


def solution(mesh):
    from jax.sharding import PartitionSpec as P

    both = ("group", "date")
    return jax.shard_map(
        on_device,
        mesh=mesh,
        in_specs=(
            P(both, None, None, None, None),
            P(both, None, None),
            P(both, None),
            P(both, None),
            P(both),
            P(both, None),
        ),
        out_specs=P(both, None, None, None),
        check_vma=False,
    )
```

```python
import functools
import math

import jax
import jax.numpy as jnp
import ml_dtypes
import numpy as np
from jax import lax
from jax.experimental import pallas as pl
from jax.experimental.pallas import tpu as pltpu

LB = 2
TAPS = 8
LOOKS = 128
ITERS = 8
PATCH = 32
LANES = 128
EPSILON = 1e-06
SHRINK = 0.05
F32 = jnp.float32
BF16 = jnp.bfloat16


def ceil_to(value, step):
    return -(-value // step) * step


def filter_tables(chunks):
    def pair(span):
        index = np.arange(span)
        product = (index[:, None] % PATCH) * (index[None, :] % PATCH) % PATCH
        angle = product.astype(np.float32) * np.float32(2.0 * math.pi / PATCH)
        inside = index[:, None] // PATCH == index[None, :] // PATCH
        return np.where(inside, np.cos(angle), 0.0), np.where(inside, np.sin(angle), 0.0)

    cosine, sine = pair(LANES)
    line_cos, line_sin = pair(PATCH)
    eye = np.eye(chunks)
    forward = np.block([[cosine, -sine], [sine, cosine]])
    inverse = np.block([[cosine, sine], [-sine, cosine]])
    lines = np.concatenate([np.kron(line_cos, eye), np.kron(line_sin, eye)], axis=1)
    return tuple(t.astype(ml_dtypes.bfloat16) for t in (forward, lines, inverse))


def dot(a, b, **kw):
    return jnp.dot(a, b, preferred_element_type=F32, **kw)


def turned(v):
    half = v.shape[0] // 2
    return jnp.concatenate([-v[half:], v[:half]], axis=0)


def resample_and_merge(x, taps, drifts, seams, prior, lines, xp, stage, send):
    bursts, sweeps, _, cells = x.shape[1:]
    depth = xp.shape[1] // 2
    chunks = cells // LANES
    xp[...] = jnp.zeros_like(xp)
    for b in range(bursts):
        for c in range(2):
            xp[b, c * depth : c * depth + sweeps, LANES : LANES + cells] = x[0, b, :, c, :].astype(F32)
    weights = taps[0].astype(F32)
    apart = (
        lax.broadcasted_iota(jnp.int32, (3 * LANES, LANES), 0)
        - lax.broadcasted_iota(jnp.int32, (3 * LANES, LANES), 1)
        - LANES
        + (TAPS // 2 - 1)
    )
    resampled = []
    for b in range(bursts):
        distance = apart - drifts[0, b]
        band = jnp.zeros((3 * LANES, LANES), F32)
        for k in range(TAPS):
            band = jnp.where(distance == k, weights[b : b + 1, k : k + 1], band)
        left = jnp.concatenate(
            [xp[b, :, k * LANES : (k + 3) * LANES] for k in range(chunks)], axis=0
        ).astype(BF16)
        resampled.append(dot(left, band.astype(BF16)).astype(BF16))
    columns = [
        jnp.concatenate(
            [r[(k * 2 + c) * depth : (k * 2 + c + 1) * depth] for r in resampled], axis=0
        )
        for c in range(2)
        for k in range(chunks)
    ]
    rows = send.shape[0]
    line = lax.broadcasted_iota(jnp.int32, (rows, bursts * depth), 0) - 1
    sweep = lax.broadcasted_iota(jnp.int32, (rows, bursts * depth), 1)
    place = jnp.zeros((rows, bursts * depth), F32)
    start = -prior[0]
    for b in range(bursts):
        if b > 0:
            start = start + sweeps - seams[0, b - 1]
        own = sweep - b * depth
        ramp = jnp.ones((rows, bursts * depth), F32)
        if b > 0:
            shared = jnp.full((1, 1), seams[0, b - 1] + 1, jnp.int32).astype(F32)
            ramp = ramp * jnp.clip((line - start + 1).astype(F32) / shared, 0.0, 1.0)
        if b < bursts - 1:
            shared = jnp.full((1, 1), seams[0, b] + 1, jnp.int32).astype(F32)
            ramp = ramp * jnp.clip((start + sweeps - line).astype(F32) / shared, 0.0, 1.0)
        here = (line == start + own) & (own >= 0) & (own < sweeps) & (line >= 0) & (line < lines)
        place = jnp.where(here, ramp, place)
    merged = dot(place.astype(BF16), jnp.concatenate(columns, axis=1))
    width = 2 * chunks
    for j in range(width):
        stage[pl.ds(j, rows, stride=width), :] = merged[:, j * LANES : (j + 1) * LANES]
    send[...] = stage[...].astype(BF16).reshape(send.shape)


def link(dates, frames, arrived, border, table, table16, gram, stage, send):
    windows = frames.shape[0]
    local_lines = arrived.shape[1]
    chunks = arrived.shape[2] // 2
    both = 2 * dates
    small = dates <= 16

    def spread(which, d, carry):
        for l in which:
            half, base = l // (local_lines // 2), (l % (local_lines // 2)) * chunks
            tile = arrived[d, l].astype(F32)
            for c in range(2):
                table[half, pl.ds(base * both + c * dates + d, chunks, stride=both), :] = tile[
                    c * chunks : (c + 1) * chunks
                ]
        return carry

    inner = functools.partial(spread, range(1, local_lines - 1))
    outer = functools.partial(spread, (0, local_lines - 1))
    lax.fori_loop(0, dates, inner, 0, unroll=small)
    border()
    lax.fori_loop(0, dates, outer, 0, unroll=small)
    for half in range(2):
        table16[:, half * LANES : (half + 1) * LANES] = table[half].astype(BF16)
    groups = local_lines // 2 * chunks
    extent = groups * LANES
    cell = lax.broadcasted_iota(jnp.int32, (2 * LANES, LOOKS), 0)

    def look(w, carry):
        frame = frames[pl.ds(w, 1), :]
        high = (frame >= extent).astype(jnp.int32)
        rest = frame - high * extent
        low = (rest & (LANES - 1)) + high * LANES
        group = rest >> 7
        hot = jnp.where(cell == low, 1.0, 0.0).astype(BF16)
        if small:
            found = dot(table16[...], hot)
            z = jnp.zeros((both, LOOKS), F32)
            for g in range(groups):
                z = jnp.where(group == g, found[g * both : (g + 1) * both], z)
        else:

            def pick(g, z):
                at = pl.ds(pl.multiple_of(g * both, both), both)
                return jnp.where(group == g, dot(table16[at, :], hot), z)

            z = lax.fori_loop(0, groups, pick, jnp.zeros((both, LOOKS), F32))
        z = jnp.concatenate([z, turned(z)], axis=1).astype(BF16)
        gram[w] = lax.dot_general(z, z, (((1,), (1,)), ((), ())), preferred_element_type=F32) * (
            1.0 / LOOKS
        )
        return carry

    lax.fori_loop(0, windows, look, 0, unroll=small)
    cov = gram[...]
    shape = (1, both, both)
    eye = lax.broadcasted_iota(jnp.int32, shape, 1) == lax.broadcasted_iota(jnp.int32, shape, 2)
    diagonal = jnp.where(eye, cov, 0.0)
    root_row = lax.rsqrt(jnp.sum(diagonal, axis=1, keepdims=True) + EPSILON)
    root_col = lax.rsqrt(jnp.sum(diagonal, axis=2, keepdims=True) + EPSILON)
    gram[...] = (1.0 - SHRINK) * cov * root_col * root_row + jnp.where(eye, SHRINK, 0.0)

    def two_steps(_, v):
        for axis in (1, 2):
            u = jnp.sum(gram[...] * v, axis=axis, keepdims=True)
            norm = jnp.sum(u * u, axis=3 - axis, keepdims=True) * (1.0 / dates)
            v = u * lax.rsqrt(norm + EPSILON)
        return v

    column = lax.broadcasted_iota(jnp.int32, (windows, both, 1), 1)
    v = jnp.where(column < dates, 1.0, 0.0).astype(F32)
    v = lax.fori_loop(0, ITERS // 2, two_steps, v, unroll=small)
    linked = v.astype(BF16).astype(F32)
    for w in range(windows):
        l, k = 1 + w // chunks, w % chunks
        half, base = l // (local_lines // 2), (l % (local_lines // 2)) * chunks
        own = table[half, (base + k) * both : (base + k + 1) * both, :]
        hist = jnp.broadcast_to(linked[w], own.shape)
        turn = turned(hist)
        scale = 1.0 / math.sqrt(dates)
        real = (jnp.sum(hist * own, axis=0, keepdims=True) * scale).astype(BF16).astype(F32)
        imag = (jnp.sum(turn * own, axis=0, keepdims=True) * scale).astype(BF16).astype(F32)
        rebuilt = real * hist + imag * turn
        for c in range(2):
            stage[pl.ds(c * windows + w, dates, stride=2 * windows), :] = rebuilt[
                c * dates : (c + 1) * dates
            ]
    send[...] = stage[...].astype(BF16).reshape(send.shape)


def patch_filter(arrived, forward, lines, inverse, stage, out):
    devices, rows = arrived.shape[0], arrived.shape[1] // 2
    chunks = rows // LB
    per = PATCH // LB
    shape = (LANES, LANES)
    same = (
        lax.broadcasted_iota(jnp.int32, shape, 0) // PATCH
        == lax.broadcasted_iota(jnp.int32, shape, 1) // PATCH
    )
    ones = jnp.where(same, 1.0 / (PATCH * PATCH), 0.0).astype(F32)

    def crossed(pair, sign):
        first, second = pair[:, :LANES], pair[:, LANES:]
        flipped = [second, -first] if sign > 0 else [-second, first]
        return jnp.concatenate([pair, jnp.concatenate(flipped, axis=1)], axis=0).astype(BF16)

    for p in range(devices // per):
        block = arrived[p * per : (p + 1) * per]
        image = jnp.concatenate(
            [block[:, c * rows : (c + 1) * rows].reshape(per * rows, LANES) for c in range(2)],
            axis=1,
        )
        first = dot(image, forward[...])
        spectrum = dot(lines[...], crossed(first, 1))
        real = spectrum[:, :LANES].reshape(PATCH, chunks, LANES)
        imag = spectrum[:, LANES:].reshape(PATCH, chunks, LANES)
        power = real * real + imag * imag
        mean = dot(jnp.sum(power, axis=0), ones, precision=lax.Precision.HIGHEST)
        ramp = jnp.sqrt(jnp.sqrt(power * (1.0 / (mean + EPSILON))[None]))
        weighted = jnp.concatenate(
            [(part * ramp).reshape(per * rows, LANES) for part in (real, imag)], axis=1
        )
        back = dot(lines[...], crossed(weighted, -1)).astype(BF16)
        filtered = dot(back, inverse[...]) * (1.0 / (PATCH * PATCH))
        for c in range(2):
            stage[c] = filtered[:, c * LANES : (c + 1) * LANES]
            for k in range(chunks):
                out[0, c, p * PATCH : (p + 1) * PATCH, k * LANES : (k + 1) * LANES] = stage[
                    c, pl.ds(k, PATCH, stride=chunks), :
                ].astype(BF16)


def kernel(
    dates, x, taps, drifts, seams, prior, frames, forward, lines, inverse, out,
    xp, stage1, send1, got1, table, table16, gram, stage2, send2, got2, stage3,
    out_sem1, in_sem1, out_sem2, in_sem2, held_forward, held_lines, held_inverse, table_sem,
    edge_out, edge_in,
):
    me = lax.axis_index("date")
    held = (held_forward, held_lines, held_inverse)
    fetches = [
        pltpu.make_async_copy(source, target, table_sem.at[i])
        for i, (source, target) in enumerate(zip((forward, lines, inverse), held))
    ]
    for fetch in fetches:
        fetch.start()
    small = dates <= 16

    def others(body):
        def step(j, carry):
            off = dates // 2 + (2 * (j % 2) - 1) * ((j + 1) // 2)
            body(off, lax.rem(me + off, dates), lax.rem(me + dates - off, dates))
            return carry

        lax.fori_loop(0, dates - 1, step, 0, unroll=small)

    barrier = pltpu.get_barrier_semaphore()
    others(
        lambda off, to, _: pl.semaphore_signal(
            barrier, inc=1, device_id={"date": to}, device_id_type=pl.DeviceIdType.MESH
        )
    )
    resample_and_merge(x, taps, drifts, seams, prior, LB * dates, xp, stage1, send1)
    pl.semaphore_wait(barrier, dates - 1)

    def landed(target, at):
        return target.at[at, pl.ds(1, LB)] if target is got1 else target.at[at]

    def copy(source, target, off, to, landing, out_sem, in_sem):
        return pltpu.make_async_remote_copy(
            src_ref=source,
            dst_ref=landed(target, landing),
            send_sem=out_sem.at[off],
            recv_sem=in_sem.at[landing],
            device_id={"date": to},
            device_id_type=pl.DeviceIdType.MESH,
        )

    def block(g):
        return send1.at[pl.ds(g * LB + 1, LB)]

    others(lambda off, to, _: copy(block(to), got1, off, to, me, out_sem1, in_sem1).start())
    got1[me, 1 : LB + 1] = send1[pl.ds(me * LB + 1, LB)]
    others(lambda off, to, src: copy(block(to), got1, off, to, src, out_sem1, in_sem1).wait_recv())

    def edge(way):
        line, landing = (LB, 0) if way else (1, LB + 1)
        to = me + 1 if way else me - 1
        return pltpu.make_async_remote_copy(
            src_ref=got1.at[:, pl.ds(line, 1)],
            dst_ref=got1.at[:, pl.ds(landing, 1)],
            send_sem=edge_out.at[way],
            recv_sem=edge_in.at[way],
            device_id={"date": to},
            device_id_type=pl.DeviceIdType.MESH,
        )

    first, last = me == 0, me == dates - 1
    pl.when(jnp.logical_not(last))(lambda: edge(1).start())
    pl.when(jnp.logical_not(first))(lambda: edge(0).start())

    def blank(line):
        got1[:, line : line + 1] = jnp.zeros((dates, 1, *got1.shape[2:]), BF16)

    def border():
        pl.when(first)(lambda: blank(0))
        pl.when(last)(lambda: blank(LB + 1))
        pl.when(jnp.logical_not(first))(lambda: edge(1).wait_recv())
        pl.when(jnp.logical_not(last))(lambda: edge(0).wait_recv())

    link(dates, frames, got1, border, table, table16, gram, stage2, send2)
    others(lambda off, to, _: copy(send2.at[to], got2, off, to, me, out_sem2, in_sem2).start())
    got2[me] = send2[me]
    others(
        lambda off, to, src: copy(send2.at[to], got2, off, to, src, out_sem2, in_sem2).wait_recv()
    )
    for fetch in fetches:
        fetch.wait()
    patch_filter(got2, *held, stage3, out)
    others(lambda off, to, _: copy(block(to), got1, off, to, me, out_sem1, in_sem1).wait_send())
    pl.when(jnp.logical_not(last))(lambda: edge(1).wait_send())
    pl.when(jnp.logical_not(first))(lambda: edge(0).wait_send())
    others(lambda off, to, _: copy(send2.at[to], got2, off, to, me, out_sem2, in_sem2).wait_send())


def on_device(records, taps, drifts, seams, prior, frames):
    dates = lax.axis_size("date")
    _, bursts, _, sweeps, cells = records.shape
    windows = frames.shape[0]
    chunks = cells // LANES
    lines = LB * dates
    rows = ceil_to(lines + 2, 8)
    depth = ceil_to(sweeps, 16)
    width = 2 * chunks
    both = 2 * dates
    groups = (LB + 2) // 2 * chunks
    vmem = pl.BlockSpec(memory_space=pltpu.VMEM)
    smem = pl.BlockSpec(memory_space=pltpu.SMEM)
    far = pl.BlockSpec(memory_space=pltpu.HBM)
    tables = [jnp.asarray(t) for t in filter_tables(chunks)]
    return pl.pallas_call(
        functools.partial(kernel, dates),
        out_shape=jax.ShapeDtypeStruct((1, 2, lines, cells), BF16),
        in_specs=[vmem, vmem, smem, smem, smem, vmem, far, far, far],
        out_specs=vmem,
        scratch_shapes=[
            pltpu.VMEM((bursts, 2 * depth, cells + 2 * LANES), F32),
            pltpu.VMEM((rows * width, LANES), F32),
            pltpu.VMEM((rows, width, LANES), BF16),
            pltpu.VMEM((dates, LB + 2, width, LANES), BF16),
            pltpu.VMEM((2, groups * both, LANES), F32),
            pltpu.VMEM((groups * both, 2 * LANES), BF16),
            pltpu.VMEM((windows, both, both), F32),
            pltpu.VMEM((both * windows, LANES), F32),
            pltpu.VMEM((dates, 2 * windows, LANES), BF16),
            pltpu.VMEM((dates, 2 * windows, LANES), BF16),
            pltpu.VMEM((2, PATCH * chunks, LANES), F32),
            pltpu.SemaphoreType.DMA((dates,)),
            pltpu.SemaphoreType.DMA((dates,)),
            pltpu.SemaphoreType.DMA((dates,)),
            pltpu.SemaphoreType.DMA((dates,)),
            *[pltpu.VMEM(t.shape, BF16) for t in tables],
            pltpu.SemaphoreType.DMA((len(tables),)),
            pltpu.SemaphoreType.DMA((2,)),
            pltpu.SemaphoreType.DMA((2,)),
        ],
        compiler_params=pltpu.CompilerParams(
            collective_id=0, has_side_effects=True, vmem_limit_bytes=55000 * 2**10
        ),
    )(jnp.swapaxes(records, 2, 3), taps, drifts, seams, prior, frames, *tables)


def solution(mesh):
    from jax.sharding import PartitionSpec as P

    both = ("group", "date")
    return jax.shard_map(
        on_device,
        mesh=mesh,
        in_specs=(
            P(both, None, None, None, None),
            P(both, None, None),
            P(both, None),
            P(both, None),
            P(both),
            P(both, None),
        ),
        out_specs=P(both, None, None, None),
        check_vma=False,
    )
```
